512 devices in a mesh: ctx: 32 (over z, x), head: 16 (over y, core).
Axes of the slice: x: 4, y: 8, z: 8, core: 2. Of those that a mesh axis runs over, the one named last changes fastest.
Arguments:
- query_proj: bfloat16 [16384, 8192], P('ctx', 'head'), may hold values from -90 to 90
- key_value: bfloat16 [16384, 2048], P('ctx', 'head'), may hold values from -90 to 90
- query_gain: float32 [128], replicated, may hold values from 0.25 to 1.75
- key_gain: float32 [128], replicated, may hold values from 0.25 to 1.75
- doc_offsets: int32 [65], replicated, may hold values from 0 to 16384, as said below
Outputs:
- attention: bfloat16 [16384, 8192], P('ctx', 'head')
The draws below stay inside these ranges and needn't reach their ends.
Inputs may be any that keep to these rules, and one draw needn't show every extreme that they name: `doc_offsets`: entry 0 is 0 and the last is 16384; entries never fall; each difference of neighbours is 0 or a multiple of 256 from 256 to 8448, the nonzero ones first, and one difference equals 8448.
All inputs are finite; a program needn't handle non-finite values.
Results may differ from the reference program's by a relative error of at most 0.0061.
Values may be sent and summed in bfloat16 or wider, within the bound.
A program may use at most 64 MiB of HBM per device.

```python
import jax
import jax.numpy as jnp
from jax import lax

HD = 128
GROUP = 8
TOK_DEV = 512
HEADS = 64
KV_HEADS = 8
TOKENS = 16384
MIN_LEN = 256
MOST_LEN = 8448
REACH = 17
DOCS = 64


def shared_rows(key, rows, cols, spread):
    noise_key = jax.random.fold_in(key, 0)
    scale_key = jax.random.fold_in(key, 2)
    noise = jax.random.truncated_normal(noise_key, -6.0, 6.0, (rows, cols), jnp.float32)
    scales = jnp.exp(jax.random.uniform(scale_key, (rows, 1), jnp.float32) * jnp.log(jnp.float32(spread)))
    mixed = jnp.sqrt(1.0) * noise
    return scales * mixed


def draw_query_proj(key, part):
    key = jax.random.fold_in(key, 1)
    return shared_rows(key, TOKENS, HEADS * HD, 1.0).astype(jnp.bfloat16)


def draw_key_value(key, part):
    key = jax.random.fold_in(key, 2)
    return shared_rows(key, TOKENS, 2 * KV_HEADS * HD, 1.0).astype(jnp.bfloat16)


def draw_doc_offsets(key, part):
    key = jax.random.fold_in(key, 3)
    length_key, slot_key = jax.random.split(key)
    units_total = TOKENS // MIN_LEN
    longest = MOST_LEN // MIN_LEN
    remaining = units_total - longest
    raw_lengths = jax.random.randint(length_key, (DOCS - 1,), 1, longest + 1, dtype=jnp.int32)
    capped = jnp.minimum(jnp.cumsum(raw_lengths), remaining)
    zero_one = jnp.zeros((1,), jnp.int32)
    pieces = capped - jnp.concatenate([zero_one, capped[:-1]])
    filled = jnp.sum((pieces > 0).astype(jnp.int32))
    slot = jax.random.randint(slot_key, (), 0, filled + 1, dtype=jnp.int32)
    index = jnp.arange(DOCS, dtype=jnp.int32)
    before = jnp.concatenate([pieces, zero_one])
    after = jnp.concatenate([zero_one, pieces])
    lengths = jnp.where(index < slot, before, jnp.where(index == slot, longest, after))
    return (jnp.concatenate([zero_one, jnp.cumsum(lengths)]) * MIN_LEN).astype(jnp.int32)


def setup_inputs(seed: int = 0) -> dict:
    key_list = jax.random.split(jax.random.key(seed), 6)
    return {
        "query_proj": draw_query_proj(jax.random.fold_in(key_list[5], 71), 0),
        "key_value": draw_key_value(jax.random.fold_in(key_list[5], 71), 0),
        "query_gain": jnp.clip(1.0 + 0.15 * jax.random.normal(key_list[2], (HD,), jnp.float32), 0.25, 1.75),
        "key_gain": jnp.clip(1.0 + 0.15 * jax.random.normal(key_list[3], (HD,), jnp.float32), 0.25, 1.75),
        "doc_offsets": draw_doc_offsets(jax.random.fold_in(key_list[5], 71), 0),
    }


norm_eps = 1e-06
rope_base = 1000000.0

def doc_starts(places, doc_offsets):
    earlier = doc_offsets[None, :] <= places[:, None]
    return lax.optimization_barrier(jnp.max(jnp.where(earlier, doc_offsets[None, :], 0), axis=1))

def rope_tables(relative, head_width):
    halves = head_width // 2
    exponent = jnp.arange(halves, dtype=jnp.float32) * (2.0 / head_width)
    frequency = jnp.exp(-exponent * jnp.log(jnp.float32(rope_base)))
    angles = relative.astype(jnp.float32)[:, None] * frequency[None, :]
    return (jnp.cos(angles), jnp.sin(angles))

def normed_rotated(projected, gain_vector, cos_table, sin_table):
    halves = projected.shape[-1] // 2
    mean_square = lax.optimization_barrier(jnp.mean(projected * projected, axis=-1, keepdims=True))
    scaled = projected * lax.rsqrt(mean_square + norm_eps) * gain_vector
    first_half = scaled[..., :halves]
    second_half = scaled[..., halves:]
    cos_rows = cos_table[:, None, :]
    sin_rows = sin_table[:, None, :]
    return jnp.concatenate([first_half * cos_rows - second_half * sin_rows, second_half * cos_rows + first_half * sin_rows], axis=-1)

def reference(query_proj, key_value, query_gain, key_gain, doc_offsets):
    places = jnp.arange(TOKENS, dtype=jnp.int32)
    starts = doc_starts(places, doc_offsets)
    cos_table, sin_table = rope_tables(places - starts, HD)
    projected = query_proj.astype(jnp.float32).reshape(TOKENS, HEADS, HD)
    queries = (normed_rotated(projected, query_gain, cos_table, sin_table) * HD ** (-0.5)).astype(jnp.bfloat16)
    paired = key_value.reshape(TOKENS, KV_HEADS, 2, HD)
    key_rows = normed_rotated(paired[:, :, 0, :].astype(jnp.float32), key_gain, cos_table, sin_table).astype(jnp.bfloat16)
    value_wide = paired[:, :, 1, :].astype(jnp.float32)
    query_wide = lax.optimization_barrier(queries).astype(jnp.float32).reshape(TOKENS // TOK_DEV, TOK_DEV, KV_HEADS, GROUP, HD)
    key_wide = lax.optimization_barrier(key_rows).astype(jnp.float32)

    def one_block(item_data):
        query_block, block_index = item_data
        first_row = block_index * TOK_DEV
        row_places = first_row + jnp.arange(TOK_DEV, dtype=jnp.int32)
        row_starts = lax.dynamic_slice_in_dim(starts, first_row, TOK_DEV, 0)

        def step_back(distance, running):
            source = block_index - distance
            key_start = jnp.maximum(source, 0) * TOK_DEV
            key_places = jnp.where(source >= 0, key_start, 4 * TOKENS) + jnp.arange(TOK_DEV, dtype=jnp.int32)
            touched = jnp.logical_and(source >= 0, jnp.logical_and(key_start <= jnp.max(row_places), key_start + TOK_DEV - 1 >= jnp.min(row_starts)))

            def compute(totals):
                numer_total, denom_total = totals
                key_block = lax.dynamic_slice_in_dim(key_wide, key_start, TOK_DEV, 0)
                value_block = lax.dynamic_slice_in_dim(value_wide, key_start, TOK_DEV, 0)
                scores = jnp.einsum('rgjd,kgd->rgjk', query_block, key_block, precision=lax.Precision.HIGHEST)
                allowed = jnp.logical_and(key_places[None, :] <= row_places[:, None], key_places[None, :] >= row_starts[:, None])
                weights = jnp.where(allowed[:, None, None, :], jnp.exp(scores), 0.0)
                denom_total = denom_total + lax.optimization_barrier(jnp.sum(weights, axis=-1))
                rounded = lax.optimization_barrier(weights.astype(jnp.bfloat16)).astype(jnp.float32)
                numer_total = numer_total + jnp.einsum('rgjk,kgd->rgjd', rounded, value_block, precision=lax.Precision.HIGHEST)
                return (numer_total, denom_total)

            def unchanged(totals):
                return totals
            return lax.cond(touched, compute, unchanged, running)
        initial = (jnp.zeros((TOK_DEV, KV_HEADS, GROUP, HD), jnp.float32), jnp.zeros((TOK_DEV, KV_HEADS, GROUP), jnp.float32))
        numerator, denominator = lax.fori_loop(0, REACH + 1, step_back, initial)
        return (numerator / denominator[..., None]).astype(jnp.bfloat16)
    blocks = lax.map(one_block, (query_wide, jnp.arange(TOKENS // TOK_DEV, dtype=jnp.int32)))
    return blocks.reshape(TOKENS, HEADS * HD)
```

```python
import functools

import jax
import jax.numpy as jnp
import numpy as np
from jax import lax
from jax.experimental import pallas as pl
from jax.experimental.pallas import tpu as pltpu
from jax.sharding import PartitionSpec as P

HD = 128
UNIT = 256
SHARD = 512
UNITS = 2
LOCAL_HEADS = 4
ROWS = LOCAL_HEADS * UNIT
X_SIZE = 4
Z_SIZE = 8
NORM_EPS = 1e-06
ROPE_BASE = 1000000.0

OWN = 0
ORDER = [
    (0, 0),
    (1, 0),
    (2, 0),
    (1, 1),
    (1, 3),
    (3, 0),
    (1, 2),
    (4, 0),
    (2, 1),
    (2, 3),
    (2, 2),
    (3, 1),
    (3, 3),
    (3, 2),
    (None, 1),
    (None, 3),
    (None, 2),
]
SLOT = {place: index for index, place in enumerate(ORDER)}
SLOTS = len(ORDER)


def rope_tables():
    frequency = ROPE_BASE ** (-np.arange(HD // 2, dtype=np.float64) * 2.0 / HD)
    sign = np.concatenate([-np.ones(HD // 2), np.ones(HD // 2)])

    def table(positions):
        angle = positions[:, None].astype(np.float64) * np.concatenate([frequency, frequency])
        return np.concatenate([np.cos(angle), np.sin(angle) * sign], axis=1).astype(np.float32)

    return table(np.arange(UNIT)), table(np.arange(64) * UNIT)


def attention_kernel(
    query_hbm,
    key_value_hbm,
    row_table_hbm,
    query_gain_ref,
    key_gain_ref,
    offsets_ref,
    base_table_ref,
    out_ref,
    query_raw,
    row_table,
    queries,
    blocks,
    totals,
    first_units,
    local_sem,
    send_sem,
    recv_sem,
    half_sem,
    pair_send_sem,
    pair_recv_sem,
):
    ctx = lax.axis_index("ctx")
    head = lax.axis_index("head")
    z, x = ctx // X_SIZE, ctx % X_SIZE
    core = head % 2

    def place(z_to, x_to):
        return (((z_to + Z_SIZE) % Z_SIZE) * X_SIZE + (x_to + X_SIZE) % X_SIZE, head)

    z_next, z_last = place(z + 1, x), place(z - 1, x)
    x_next, x_last, x_across = place(z, x + 1), place(z, x - 1), place(z, x + 2)
    partner = (ctx, head + 1 - 2 * core)

    barrier = pltpu.get_barrier_semaphore()
    for other in (partner, x_next, x_last, z_next, z_last, x_across):
        pl.semaphore_signal(barrier, inc=1, device_id=other, device_id_type=pl.DeviceIdType.MESH)

    own_rows = pl.ds(0, SHARD)
    fetch_own = pltpu.make_async_copy(key_value_hbm, blocks.at[core, own_rows], local_sem.at[0])
    fetch_own.start()
    fetch_table = pltpu.make_async_copy(row_table_hbm, row_table, local_sem.at[1])
    fetch_table.start()
    fetch_query = pltpu.make_async_copy(query_hbm, query_raw, local_sem.at[2])
    fetch_query.start()

    doc_units = []
    for unit in range(UNITS):
        first = (ctx * UNITS + unit) * UNIT
        start = 0
        for entry in range(offsets_ref.shape[0]):
            offset = offsets_ref[entry]
            start = jnp.maximum(start, jnp.where(offset <= first, offset, 0))
        doc_units.append(start // UNIT)

    for index, (row, step) in enumerate(ORDER):
        if row is None:
            shard = jnp.where(x >= step, ctx - step, ctx - 4 * X_SIZE - step + X_SIZE)
        else:
            shard = ctx - row * X_SIZE - step + jnp.where(x >= step, 0, X_SIZE)
        first_units[index] = shard * UNITS

    fetch_table.wait()

    def unit_tables(unit):
        behind = ctx * UNITS + unit - doc_units[unit]
        base = base_table_ref[pl.ds(behind, 1), :]
        base_cos, base_sin = base[:, :HD], base[:, HD:]
        row_cos, row_sin = row_table[:, :HD], row_table[:, HD:]
        cosines = base_cos * row_cos - base_sin * row_sin
        sines = base_sin * row_cos + base_cos * row_sin
        return cosines, sines

    tables = [unit_tables(unit) for unit in range(UNITS)]

    def with_gain(unit, gain_ref):
        gain = gain_ref[...].reshape(1, HD)
        cosines, sines = tables[unit]
        return cosines * gain, sines * pltpu.roll(gain, HD // 2, 1)

    def norm_rotate(rows, gained, scale):
        wide = rows.astype(jnp.float32)
        mean_square = jnp.mean(wide * wide, axis=1, keepdims=True)
        factor = lax.rsqrt(mean_square + NORM_EPS)
        if scale is not None:
            factor = factor * scale
        turned = wide * gained[0] + pltpu.roll(wide, HD // 2, 1) * gained[1]
        return (turned * factor).astype(jnp.bfloat16)

    fetch_own.wait()

    @pl.when(core == 0)
    def _():
        for unit in range(UNITS):
            rows = slice(unit * UNIT, (unit + 1) * UNIT)
            blocks[0, rows, :] = norm_rotate(
                blocks[0, rows, :], with_gain(unit, key_gain_ref), None
            )

    pl.semaphore_wait(barrier, 6)

    def rows_of(slot, half=None):
        if half is None:
            return pl.ds(slot * SHARD, SHARD)
        return pl.ds(slot * SHARD + half * UNIT, UNIT)

    send_count = [0]
    sends = []

    def to_chip(source, target, device, sem, half=None):
        arrival = recv_sem.at[target] if half is None or half == 0 else half_sem.at[target]
        return pltpu.make_async_remote_copy(
            src_ref=blocks.at[core, rows_of(source, half)],
            dst_ref=blocks.at[core, rows_of(target, half)],
            send_sem=send_sem.at[sem],
            recv_sem=arrival,
            device_id=device,
            device_id_type=pl.DeviceIdType.MESH,
        )

    def to_partner(slot):
        return pltpu.make_async_remote_copy(
            src_ref=blocks.at[core, rows_of(slot)],
            dst_ref=blocks.at[core, rows_of(slot)],
            send_sem=pair_send_sem.at[slot],
            recv_sem=pair_recv_sem.at[slot],
            device_id=partner,
            device_id_type=pl.DeviceIdType.MESH,
        )

    def from_partner(slot):
        return pltpu.make_async_remote_copy(
            src_ref=blocks.at[1 - core, rows_of(slot)],
            dst_ref=blocks.at[1 - core, rows_of(slot)],
            send_sem=pair_send_sem.at[slot],
            recv_sem=pair_recv_sem.at[slot],
            device_id=partner,
            device_id_type=pl.DeviceIdType.MESH,
        )

    def send(source, target, device, half=None):
        sem = send_count[0]
        send_count[0] += 1
        to_chip(source, target, device, sem, half).start()
        sends.append((source, target, device, sem, half))

    ahead = {1: x_next, 2: x_across, 3: x_last}
    corner = {}
    for step in (1, 3, 2):
        sem = send_count[0]
        send_count[0] += 1
        corner[step] = sem

    def to_corner(source, step):
        return to_chip(source, SLOT[(None, step)], ahead[step], corner[step])

    def arrived(slot):
        row, step = ORDER[slot]
        if row is not None and step == 2:
            for half in range(2):
                to_chip(slot, slot, x_next, 0, half).wait_recv()
        else:
            to_chip(slot, slot, x_next, 0).wait_recv()
        if row is not None:
            if step == 0:
                if row < 4:
                    send(slot, SLOT[(row + 1, 0)], z_next)
                    send(slot, SLOT[(row, 1)], x_next)
                    send(slot, SLOT[(row, 3)], x_last)
                else:
                    for corner_step in (1, 3, 2):

                        @pl.when(x + corner_step >= X_SIZE)
                        def _():
                            to_corner(SLOT[(4, 0)], corner_step).start()

            if step == 1:
                send(slot, SLOT[(row, 2)], x_next, half=0)
            if step == 3:
                send(slot, SLOT[(row, 2)], x_last, half=1)
        to_partner(slot).start()

    send(OWN, SLOT[(1, 0)], z_next)
    for corner_step in (1, 3, 2):

        @pl.when(x + corner_step < X_SIZE)
        def _():
            to_corner(OWN, corner_step).start()

    to_partner(OWN).start()

    fetch_query.wait()
    for unit in range(UNITS):
        gained = with_gain(unit, query_gain_ref)
        for local in range(LOCAL_HEADS):
            rows = query_raw[
                unit * UNIT : (unit + 1) * UNIT, local * HD : (local + 1) * HD
            ]
            queries[unit, local * UNIT : (local + 1) * UNIT, :] = norm_rotate(
                rows, gained, HD**-0.5
            )

    def scores(unit, part, part_rows, keys):
        return lax.dot_general(
            queries[unit, part * part_rows : (part + 1) * part_rows, :],
            keys,
            (((1,), (1,)), ((), ())),
            preferred_element_type=jnp.float32,
        )

    def masked_values(values, allowed):
        zero = jnp.zeros_like(values)
        return jnp.concatenate(
            [jnp.where(allowed, values, zero), jnp.where(allowed, zero + 1, zero)], axis=1
        )

    from_partner(OWN).wait_recv()
    own_first = ctx * UNITS
    for unit in range(UNITS):
        count = (unit + 1) * UNIT
        keys = blocks[0, :count, :]
        unit_of_key = own_first + lax.broadcasted_iota(jnp.int32, (count, HD), 0) // UNIT
        values = masked_values(blocks[1, :count, :], unit_of_key >= doc_units[unit])
        part_rows = 512
        for part in range(ROWS // part_rows):
            shape = (part_rows, count)
            position = lax.broadcasted_iota(jnp.int32, shape, 0) % UNIT + unit * UNIT
            causal = lax.broadcasted_iota(jnp.int32, shape, 1) <= position
            weights = jnp.where(
                causal, jnp.exp(scores(unit, part, part_rows, keys)), 0.0
            ).astype(jnp.bfloat16)
            totals[unit, part * part_rows : (part + 1) * part_rows, :] = jnp.dot(
                weights, values, preferred_element_type=jnp.float32
            )

    def attend(slot, width):
        count = width * SHARD
        at = pl.ds(pl.multiple_of(slot * SHARD, SHARD), count)
        keys = blocks[0, at, :]
        values = blocks[1, at, :]
        row = lax.broadcasted_iota(jnp.int32, (SHARD, HD), 0) // UNIT
        key_unit = jnp.concatenate(
            [row + first_units[slot + place] for place in range(width)], axis=0
        )
        masked = [masked_values(values, key_unit >= doc_units[unit]) for unit in range(UNITS)]
        part_rows = 512
        parts = [(unit, part) for unit in range(UNITS) for part in range(ROWS // part_rows)]
        held = scores(*parts[0], part_rows, keys)
        for index, (unit, part) in enumerate(parts):
            later = None
            if index + 1 < len(parts):
                later = scores(*parts[index + 1], part_rows, keys)
            weights = jnp.exp(held).astype(jnp.bfloat16)
            totals[unit, part * part_rows : (part + 1) * part_rows, :] += jnp.dot(
                weights, masked[unit], preferred_element_type=jnp.float32
            )
            held = later

    def wait_partner(slot, width):
        for place in range(width):
            from_partner(slot + place).wait_recv()

    single_events = {1: [(1, 0)], 2: [(2, 0)]}
    pair_events = {
        0: [(1, 1), (1, 3)],
        1: [(3, 0), (1, 2)],
        2: [(4, 0), (2, 1), (2, 3)],
        3: [(2, 2)],
        4: [(3, 1), (3, 3)],
        5: [(3, 2), (None, 1)],
        6: [(None, 3), (None, 2)],
    }

    def single(slot, carry):
        for index, places in single_events.items():

            @pl.when(slot == index)
            def _():
                for where in places:
                    arrived(SLOT[where])

        wait_partner(slot, 1)
        attend(slot, 1)
        return carry

    lax.fori_loop(1, 3, single, 0)

    def pair(step, carry):
        for index, places in pair_events.items():

            @pl.when(step == index)
            def _():
                for where in places:
                    arrived(SLOT[where])

        slot = 3 + 2 * step
        wait_partner(slot, 2)
        attend(slot, 2)
        return carry

    lax.fori_loop(0, 7, pair, 0)

    for unit in range(UNITS):
        for local in range(LOCAL_HEADS):
            rows = slice(local * UNIT, (local + 1) * UNIT)
            out_ref[unit * UNIT : (unit + 1) * UNIT, local * HD : (local + 1) * HD] = (
                totals[unit, rows, :HD] / totals[unit, rows, HD:]
            ).astype(jnp.bfloat16)

    for copy in sends:
        to_chip(*copy).wait_send()
    for step in (1, 3, 2):
        to_corner(OWN, step).wait_send()
    for slot in range(SLOTS):
        to_partner(slot).wait_send()


def per_device(query_proj, key_value, query_gain, key_gain, doc_offsets):
    row_table, base_table = rope_tables()
    any_space = pl.BlockSpec(memory_space=pl.ANY)
    vmem = pl.BlockSpec(memory_space=pltpu.VMEM)
    return pl.pallas_call(
        attention_kernel,
        out_shape=jax.ShapeDtypeStruct((SHARD, LOCAL_HEADS * HD), jnp.bfloat16),
        in_specs=[
            any_space,
            any_space,
            any_space,
            vmem,
            vmem,
            pl.BlockSpec(memory_space=pltpu.SMEM),
            vmem,
        ],
        out_specs=vmem,
        scratch_shapes=[
            pltpu.VMEM((SHARD, LOCAL_HEADS * HD), jnp.bfloat16),
            pltpu.VMEM((UNIT, 2 * HD), jnp.float32),
            pltpu.VMEM((UNITS, ROWS, HD), jnp.bfloat16),
            pltpu.VMEM((2, SLOTS * SHARD, HD), jnp.bfloat16),
            pltpu.VMEM((UNITS, ROWS, 2 * HD), jnp.float32),
            pltpu.SMEM((SLOTS,), jnp.int32),
            pltpu.SemaphoreType.DMA((3,)),
            pltpu.SemaphoreType.DMA((24,)),
            pltpu.SemaphoreType.DMA((SLOTS,)),
            pltpu.SemaphoreType.DMA((SLOTS,)),
            pltpu.SemaphoreType.DMA((SLOTS,)),
            pltpu.SemaphoreType.DMA((SLOTS,)),
        ],
        compiler_params=pltpu.CompilerParams(
            collective_id=0, has_side_effects=True, vmem_limit_bytes=48 * 1024 * 1024
        ),
        cost_estimate=pl.CostEstimate(
            flops=2 * 2 * 2048 * 8448 * HD, bytes_accessed=2 << 20, transcendentals=2048 * 8448
        ),
    )(
        query_proj,
        key_value,
        jnp.asarray(row_table),
        query_gain,
        key_gain,
        doc_offsets,
        jnp.asarray(base_table),
    )


def solution(mesh):
    placed = (P("ctx", "head"), P("ctx", "head"), P(), P(), P())
    return jax.shard_map(
        per_device, mesh=mesh, in_specs=placed, out_specs=P("ctx", "head"), check_vma=False
    )
```

```python
import functools

import jax
import jax.numpy as jnp
import numpy as np
from jax import lax
from jax.experimental import pallas as pl
from jax.experimental.pallas import tpu as pltpu
from jax.sharding import PartitionSpec as P

HD = 128
UNIT = 256
SHARD = 512
UNITS = 2
LOCAL_HEADS = 4
ROWS = LOCAL_HEADS * UNIT
X_SIZE = 4
Z_SIZE = 8
NORM_EPS = 1e-06
ROPE_BASE = 1000000.0

OWN = 0
ORDER = [
    (0, 0),
    (1, 0),
    (2, 0),
    (1, 1),
    (1, 3),
    (3, 0),
    (1, 2),
    (2, 1),
    (2, 3),
    (4, 0),
    (2, 2),
    (3, 1),
    (3, 3),
    (3, 2),
    (None, 1),
    (None, 3),
    (None, 2),
]
SLOT = {place: index for index, place in enumerate(ORDER)}
SLOTS = len(ORDER)


def rope_tables():
    frequency = ROPE_BASE ** (-np.arange(HD // 2, dtype=np.float64) * 2.0 / HD)
    sign = np.concatenate([-np.ones(HD // 2), np.ones(HD // 2)])

    def table(positions):
        angle = positions[:, None].astype(np.float64) * np.concatenate([frequency, frequency])
        return np.concatenate([np.cos(angle), np.sin(angle) * sign], axis=1).astype(np.float32)

    return table(np.arange(UNIT)), table(np.arange(64) * UNIT)


def attention_kernel(
    query_hbm,
    key_value_hbm,
    row_table_hbm,
    query_gain_hbm,
    key_gain_hbm,
    offsets_hbm,
    base_table_hbm,
    out_ref,
    query_raw,
    row_table,
    query_gain_ref,
    key_gain_ref,
    offsets_ref,
    base_table_ref,
    queries,
    blocks,
    totals,
    first_units,
    local_sem,
    send_sem,
    recv_sem,
    half_sem,
    pair_send_sem,
    pair_recv_sem,
):
    ctx = lax.axis_index("ctx")
    head = lax.axis_index("head")
    z, x = ctx // X_SIZE, ctx % X_SIZE
    core = head % 2

    def place(z_to, x_to):
        return (((z_to + Z_SIZE) % Z_SIZE) * X_SIZE + (x_to + X_SIZE) % X_SIZE, head)

    z_next, z_last = place(z + 1, x), place(z - 1, x)
    x_next, x_last, x_across = place(z, x + 1), place(z, x - 1), place(z, x + 2)
    partner = (ctx, head + 1 - 2 * core)

    barrier = pltpu.get_barrier_semaphore()

    def greet(other):
        pl.semaphore_signal(barrier, inc=1, device_id=other, device_id_type=pl.DeviceIdType.MESH)

    @pl.when(z > 0)
    def _():
        greet(z_last)

    @pl.when(z < Z_SIZE - 1)
    def _():
        greet(z_next)

    for other in (x_next, x_last, x_across, partner):
        greet(other)

    own_rows = pl.ds(0, SHARD)
    fetches = [
        pltpu.make_async_copy(source, target, local_sem.at[index])
        for index, (source, target) in enumerate(
            (
                (offsets_hbm, offsets_ref),
                (base_table_hbm, base_table_ref),
                (key_gain_hbm, key_gain_ref),
                (key_value_hbm, blocks.at[core, own_rows]),
                (row_table_hbm, row_table),
                (query_gain_hbm, query_gain_ref),
                (query_hbm, query_raw),
            )
        )
    ]
    for fetch in fetches:
        fetch.start()
    fetch_offsets, fetch_base, fetch_key_gain, fetch_own, fetch_table, fetch_gain, fetch_query = fetches

    fetch_offsets.wait()
    doc_units = []
    for unit in range(UNITS):
        first = (ctx * UNITS + unit) * UNIT
        start = 0
        for entry in range(offsets_ref.shape[0]):
            offset = offsets_ref[entry]
            start = jnp.maximum(start, jnp.where(offset <= first, offset, 0))
        doc_units.append(start // UNIT)

    for index, (row, step) in enumerate(ORDER):
        if row is None:
            shard = jnp.where(x >= step, ctx - step, ctx - 4 * X_SIZE - step + X_SIZE)
        else:
            shard = ctx - row * X_SIZE - step + jnp.where(x >= step, 0, X_SIZE)
        first_units[index] = shard * UNITS

    fetch_base.wait()
    fetch_key_gain.wait()
    fetch_table.wait()

    def unit_tables(unit):
        behind = ctx * UNITS + unit - doc_units[unit]
        base = base_table_ref[pl.ds(behind, 1), :]
        base_cos, base_sin = base[:, :HD], base[:, HD:]
        row_cos, row_sin = row_table[:, :HD], row_table[:, HD:]
        cosines = base_cos * row_cos - base_sin * row_sin
        sines = base_sin * row_cos + base_cos * row_sin
        return cosines, sines

    tables = [unit_tables(unit) for unit in range(UNITS)]

    def with_gain(unit, gain_ref):
        gain = gain_ref[...].reshape(1, HD)
        cosines, sines = tables[unit]
        return cosines * gain, sines * pltpu.roll(gain, HD // 2, 1)

    def norm_rotate(rows, gained, scale):
        wide = rows.astype(jnp.float32)
        mean_square = jnp.mean(wide * wide, axis=1, keepdims=True)
        factor = lax.rsqrt(mean_square + NORM_EPS)
        if scale is not None:
            factor = factor * scale
        turned = wide * gained[0] + pltpu.roll(wide, HD // 2, 1) * gained[1]
        return (turned * factor).astype(jnp.bfloat16)

    fetch_own.wait()

    @pl.when(core == 0)
    def _():
        for unit in range(UNITS):
            rows = slice(unit * UNIT, (unit + 1) * UNIT)
            blocks[0, rows, :] = norm_rotate(
                blocks[0, rows, :], with_gain(unit, key_gain_ref), None
            )

    def rows_of(slot, half=None):
        if half is None:
            return pl.ds(slot * SHARD, SHARD)
        return pl.ds(slot * SHARD + half * UNIT, UNIT)

    def holds(slot):
        row, step = ORDER[slot]
        if row is None:
            return jnp.logical_or(x >= step, z >= 4)
        return z >= row

    for slot in range(1, SLOTS):

        @pl.when(jnp.logical_not(holds(slot)))
        def _():
            blocks[0, rows_of(slot), :] = jnp.zeros((SHARD, HD), jnp.bfloat16)

    pl.semaphore_wait(
        barrier, 4 + jnp.where(z > 0, 1, 0) + jnp.where(z < Z_SIZE - 1, 1, 0)
    )

    def to_chip(source, target, device, sem, half=None):
        arrival = half_sem.at[target] if half == 1 else recv_sem.at[target]
        return pltpu.make_async_remote_copy(
            src_ref=blocks.at[core, rows_of(source, half)],
            dst_ref=blocks.at[core, rows_of(target, half)],
            send_sem=send_sem.at[sem],
            recv_sem=arrival,
            device_id=device,
            device_id_type=pl.DeviceIdType.MESH,
        )

    def to_partner(slot):
        return pltpu.make_async_remote_copy(
            src_ref=blocks.at[core, rows_of(slot)],
            dst_ref=blocks.at[core, rows_of(slot)],
            send_sem=pair_send_sem.at[slot],
            recv_sem=pair_recv_sem.at[slot],
            device_id=partner,
            device_id_type=pl.DeviceIdType.MESH,
        )

    def from_partner(slot):
        return pltpu.make_async_remote_copy(
            src_ref=blocks.at[1 - core, rows_of(slot)],
            dst_ref=blocks.at[1 - core, rows_of(slot)],
            send_sem=pair_send_sem.at[slot],
            recv_sem=pair_recv_sem.at[slot],
            device_id=partner,
            device_id_type=pl.DeviceIdType.MESH,
        )

    sends = []

    def plan(source, target, device, half, condition):
        sends.append((source, target, device, half, condition))

    ahead = {1: x_next, 2: x_across, 3: x_last}
    below = z < Z_SIZE - 1
    for half in range(2):
        plan(OWN, SLOT[(1, 0)], z_next, half, below)
    for step in (1, 3, 2):
        plan(OWN, SLOT[(None, step)], ahead[step], None, x + step < X_SIZE)
    for row in (1, 2, 3):
        have = z >= row
        slot = SLOT[(row, 0)]
        for half in range(2):
            plan(slot, SLOT[(row + 1, 0)], z_next, half, jnp.logical_and(have, below))
            plan(slot, SLOT[(row, 1)], x_next, half, have)
            plan(slot, SLOT[(row, 3)], x_last, half, have)
        plan(SLOT[(row, 1)], SLOT[(row, 2)], x_next, 0, have)
        plan(SLOT[(row, 3)], SLOT[(row, 2)], x_last, 1, have)
    for step in (1, 3, 2):
        condition = jnp.logical_and(x + step >= X_SIZE, z >= 4)
        plan(SLOT[(4, 0)], SLOT[(None, step)], ahead[step], None, condition)

    def send_from(slot, halves):
        for sem, (source, target, device, half, condition) in enumerate(sends):
            if source == slot and half in halves:

                @pl.when(condition)
                def _():
                    to_chip(source, target, device, sem, half).start()

    def arrived(place, half=None):
        slot = SLOT[place]
        if place[0] is None:
            halves = (None,)
        elif half is None:
            halves = (0, 1)
        else:
            halves = (half,)

        @pl.when(holds(slot))
        def _():
            for part in halves:
                to_chip(slot, slot, x_next, 0, part).wait_recv()
            if halves[-1] != 0:
                to_partner(slot).start()

        send_from(slot, halves + (None,) if halves[-1] == 1 else halves)

    def wait_partner(slot):
        @pl.when(holds(slot))
        def _():
            from_partner(slot).wait_recv()

    to_partner(OWN).start()
    send_from(OWN, (None, 0, 1))

    fetch_gain.wait()
    fetch_query.wait()

    def prepare_queries(unit):
        gained = with_gain(unit, query_gain_ref)
        for local in range(LOCAL_HEADS):
            rows = query_raw[
                unit * UNIT : (unit + 1) * UNIT, local * HD : (local + 1) * HD
            ]
            queries[unit, local * UNIT : (local + 1) * UNIT, :] = norm_rotate(
                rows, gained, HD**-0.5
            )

    def scores(unit, part, part_rows, keys):
        return lax.dot_general(
            queries[unit, part * part_rows : (part + 1) * part_rows, :],
            keys,
            (((1,), (1,)), ((), ())),
            preferred_element_type=jnp.float32,
        )

    def masked_values(values, allowed):
        zero = jnp.zeros_like(values)
        return jnp.concatenate(
            [jnp.where(allowed, values, zero), jnp.where(allowed, zero + 1, zero)], axis=1
        )

    own_first = ctx * UNITS

    def attend_own(unit):
        count = (unit + 1) * UNIT
        keys = blocks[0, :count, :]
        unit_of_key = own_first + lax.broadcasted_iota(jnp.int32, (count, HD), 0) // UNIT
        values = masked_values(blocks[1, :count, :], unit_of_key >= doc_units[unit])
        part_rows = 512
        for part in range(ROWS // part_rows):
            shape = (part_rows, count)
            position = lax.broadcasted_iota(jnp.int32, shape, 0) % UNIT + unit * UNIT
            causal = lax.broadcasted_iota(jnp.int32, shape, 1) <= position
            weights = jnp.where(
                causal, jnp.exp(scores(unit, part, part_rows, keys)), 0.0
            ).astype(jnp.bfloat16)
            totals[unit, part * part_rows : (part + 1) * part_rows, :] = jnp.dot(
                weights, values, preferred_element_type=jnp.float32
            )

    prepare_queries(0)
    prepare_queries(1)
    from_partner(OWN).wait_recv()
    attend_own(0)
    arrived((1, 0), 0)
    attend_own(1)
    arrived((1, 0), 1)

    def attend(slot, width):
        count = width * SHARD
        at = pl.ds(pl.multiple_of(slot * SHARD, SHARD), count)
        keys = blocks[0, at, :]
        values = blocks[1, at, :]
        row = lax.broadcasted_iota(jnp.int32, (SHARD, HD), 0) // UNIT
        key_unit = jnp.concatenate(
            [row + first_units[slot + place] for place in range(width)], axis=0
        )
        masked = [masked_values(values, key_unit >= doc_units[unit]) for unit in range(UNITS)]
        part_rows = 512
        parts = [(unit, part) for unit in range(UNITS) for part in range(ROWS // part_rows)]
        held = scores(*parts[0], part_rows, keys)
        for index, (unit, part) in enumerate(parts):
            later = None
            if index + 1 < len(parts):
                later = scores(*parts[index + 1], part_rows, keys)
            weights = jnp.exp(held).astype(jnp.bfloat16)
            totals[unit, part * part_rows : (part + 1) * part_rows, :] += jnp.dot(
                weights, masked[unit], preferred_element_type=jnp.float32
            )
            held = later

    single_events = {
        1: [((2, 0), 0), ((2, 0), 1)],
        2: [((1, 1), 0), ((1, 3), 0), ((1, 1), 1), ((1, 3), 1)],
        3: [((3, 0), 0), ((3, 0), 1)],
        4: [((1, 2),)],
    }
    pair_events = {
        0: [((2, 1),), ((2, 3),), ((4, 0),)],
        1: [((2, 2),)],
        2: [((3, 1),), ((3, 3),)],
        3: [((3, 2),), ((None, 1),)],
        4: [((None, 3),), ((None, 2),)],
        5: [],
    }
    singles = len(single_events)

    def take(step, events, first, width):
        for index, arrivals in events.items():

            @pl.when(step == index)
            def _():
                for arrival in arrivals:
                    arrived(*arrival)
                for place in range(width):
                    wait_partner(first + width * index + place)

    def single(step, carry):
        take(step, single_events, 0, 1)
        attend(step, 1)
        return carry

    lax.fori_loop(1, 1 + singles, single, 0)

    def pair(step, carry):
        take(step, pair_events, 1 + singles, 2)
        attend(1 + singles + 2 * step, 2)
        return carry

    lax.fori_loop(0, len(pair_events), pair, 0)

    for unit in range(UNITS):
        for local in range(LOCAL_HEADS):
            rows = slice(local * UNIT, (local + 1) * UNIT)
            out_ref[unit * UNIT : (unit + 1) * UNIT, local * HD : (local + 1) * HD] = (
                totals[unit, rows, :HD] / totals[unit, rows, HD:]
            ).astype(jnp.bfloat16)

    for sem, (source, target, device, half, condition) in enumerate(sends):

        @pl.when(condition)
        def _():
            to_chip(source, target, device, sem, half).wait_send()

    for slot in range(SLOTS):

        @pl.when(holds(slot))
        def _():
            to_partner(slot).wait_send()


def per_device(query_proj, key_value, query_gain, key_gain, doc_offsets):
    row_table, base_table = rope_tables()
    return pl.pallas_call(
        attention_kernel,
        out_shape=jax.ShapeDtypeStruct((SHARD, LOCAL_HEADS * HD), jnp.bfloat16),
        in_specs=[pl.BlockSpec(memory_space=pltpu.HBM)] * 7,
        out_specs=pl.BlockSpec(memory_space=pltpu.VMEM),
        scratch_shapes=[
            pltpu.VMEM((SHARD, LOCAL_HEADS * HD), jnp.bfloat16),
            pltpu.VMEM((UNIT, 2 * HD), jnp.float32),
            pltpu.VMEM((HD,), jnp.float32),
            pltpu.VMEM((HD,), jnp.float32),
            pltpu.SMEM(doc_offsets.shape, jnp.int32),
            pltpu.VMEM((64, 2 * HD), jnp.float32),
            pltpu.VMEM((UNITS, ROWS, HD), jnp.bfloat16),
            pltpu.VMEM((2, SLOTS * SHARD, HD), jnp.bfloat16),
            pltpu.VMEM((UNITS, ROWS, 2 * HD), jnp.float32),
            pltpu.SMEM((SLOTS,), jnp.int32),
            pltpu.SemaphoreType.DMA((7,)),
            pltpu.SemaphoreType.DMA((40,)),
            pltpu.SemaphoreType.DMA((SLOTS,)),
            pltpu.SemaphoreType.DMA((SLOTS,)),
            pltpu.SemaphoreType.DMA((SLOTS,)),
            pltpu.SemaphoreType.DMA((SLOTS,)),
        ],
        compiler_params=pltpu.CompilerParams(
            collective_id=0, has_side_effects=True, vmem_limit_bytes=64 * 1024 * 1024
        ),
        cost_estimate=pl.CostEstimate(
            flops=2 * 2 * 2048 * 8448 * HD, bytes_accessed=2 << 20, transcendentals=2048 * 8448
        ),
    )(
        query_proj,
        key_value,
        jnp.asarray(row_table),
        query_gain,
        key_gain,
        doc_offsets,
        jnp.asarray(base_table),
    )


def solution(mesh):
    placed = (P("ctx", "head"), P("ctx", "head"), P(), P(), P())
    return jax.shard_map(
        per_device, mesh=mesh, in_specs=placed, out_specs=P("ctx", "head"), check_vma=False
    )
```

```python
import functools

import jax
import jax.numpy as jnp
import numpy as np
from jax import lax
from jax.experimental import pallas as pl
from jax.experimental.pallas import tpu as pltpu
from jax.sharding import PartitionSpec as P

HD = 128
UNIT = 256
SHARD = 512
UNITS = 2
LOCAL_HEADS = 4
ROWS = LOCAL_HEADS * UNIT
X_SIZE = 4
Z_SIZE = 8
NORM_EPS = 1e-06
ROPE_BASE = 1000000.0

OWN = 0
ORDER = [
    (0, 0),
    (1, 0),
    (2, 0),
    (3, 0),
    (1, 1),
    (1, 3),
    (4, 0),
    (2, 3),
    (2, 1),
    (1, 2),
    (3, 3),
    (3, 1),
    (2, 2),
    (None, 1),
    (3, 2),
    (None, 3),
    (None, 2),
]
EARLY = [((1, 0), 0), ((1, 0), 1), ((2, 0), 0), ((2, 0), 1)]
ALONG_Z = ((3, 2), (2, 2), (3, 1))
SLOT = {place: index for index, place in enumerate(ORDER)}
SLOTS = len(ORDER)


def rope_tables():
    frequency = ROPE_BASE ** (-np.arange(HD // 2, dtype=np.float64) * 2.0 / HD)
    sign = np.concatenate([-np.ones(HD // 2), np.ones(HD // 2)])

    def table(positions):
        angle = positions[:, None].astype(np.float64) * np.concatenate([frequency, frequency])
        return np.concatenate([np.cos(angle), np.sin(angle) * sign], axis=1).astype(np.float32)

    return table(np.arange(UNIT)), table(np.arange(64) * UNIT)


def attention_kernel(
    query_hbm,
    key_value_hbm,
    row_table_hbm,
    query_gain_hbm,
    key_gain_hbm,
    offsets_hbm,
    base_table_hbm,
    out_ref,
    query_raw,
    row_table,
    query_gain_ref,
    key_gain_ref,
    offsets_ref,
    base_table_ref,
    queries,
    blocks,
    totals,
    first_units,
    local_sem,
    send_sem,
    recv_sem,
    half_sem,
    pair_send_sem,
    pair_recv_sem,
):
    ctx = lax.axis_index("ctx")
    head = lax.axis_index("head")
    z, x = ctx // X_SIZE, ctx % X_SIZE
    core = head % 2

    def place(z_to, x_to):
        return (((z_to + Z_SIZE) % Z_SIZE) * X_SIZE + (x_to + X_SIZE) % X_SIZE, head)

    z_next, z_last = place(z + 1, x), place(z - 1, x)
    x_next, x_last, x_across = place(z, x + 1), place(z, x - 1), place(z, x + 2)
    partner = (ctx, head + 1 - 2 * core)

    barrier = pltpu.get_barrier_semaphore()

    def greet(other):
        pl.semaphore_signal(barrier, inc=1, device_id=other, device_id_type=pl.DeviceIdType.MESH)

    @pl.when(z > 0)
    def _():
        greet(z_last)

    @pl.when(z < Z_SIZE - 1)
    def _():
        greet(z_next)

    for other in (x_next, x_last, x_across, partner):
        greet(other)

    own_rows = pl.ds(0, SHARD)
    fetches = [
        pltpu.make_async_copy(source, target, local_sem.at[index])
        for index, (source, target) in enumerate(
            (
                (offsets_hbm, offsets_ref),
                (base_table_hbm, base_table_ref),
                (key_gain_hbm, key_gain_ref),
                (key_value_hbm, blocks.at[core, own_rows]),
                (row_table_hbm, row_table),
                (query_gain_hbm, query_gain_ref),
                (query_hbm, query_raw),
            )
        )
    ]
    for fetch in fetches:
        fetch.start()
    fetch_offsets, fetch_base, fetch_key_gain, fetch_own, fetch_table, fetch_gain, fetch_query = fetches

    fetch_offsets.wait()
    doc_units = []
    for unit in range(UNITS):
        first = (ctx * UNITS + unit) * UNIT
        start = 0
        for entry in range(offsets_ref.shape[0]):
            offset = offsets_ref[entry]
            start = jnp.maximum(start, jnp.where(offset <= first, offset, 0))
        doc_units.append(start // UNIT)

    for index, (row, step) in enumerate(ORDER):
        if row is None:
            shard = jnp.where(x >= step, ctx - step, ctx - 4 * X_SIZE - step + X_SIZE)
        else:
            shard = ctx - row * X_SIZE - step + jnp.where(x >= step, 0, X_SIZE)
        first_units[index] = shard * UNITS

    fetch_base.wait()
    fetch_key_gain.wait()
    fetch_table.wait()

    def unit_tables(unit):
        behind = ctx * UNITS + unit - doc_units[unit]
        base = base_table_ref[pl.ds(behind, 1), :]
        base_cos, base_sin = base[:, :HD], base[:, HD:]
        row_cos, row_sin = row_table[:, :HD], row_table[:, HD:]
        cosines = base_cos * row_cos - base_sin * row_sin
        sines = base_sin * row_cos + base_cos * row_sin
        return cosines, sines

    tables = [unit_tables(unit) for unit in range(UNITS)]

    def with_gain(unit, gain_ref):
        gain = gain_ref[...].reshape(1, HD)
        cosines, sines = tables[unit]
        return cosines * gain, sines * pltpu.roll(gain, HD // 2, 1)

    def norm_rotate(rows, gained, scale):
        wide = rows.astype(jnp.float32)
        mean_square = jnp.mean(wide * wide, axis=1, keepdims=True)
        factor = lax.rsqrt(mean_square + NORM_EPS)
        if scale is not None:
            factor = factor * scale
        turned = wide * gained[0] + pltpu.roll(wide, HD // 2, 1) * gained[1]
        return (turned * factor).astype(jnp.bfloat16)

    def rows_of(slot, half=None):
        if half is None:
            return pl.ds(slot * SHARD, SHARD)
        return pl.ds(slot * SHARD + half * UNIT, UNIT)

    def holds(slot):
        row, step = ORDER[slot]
        if row is None:
            return jnp.logical_or(x >= step, z >= 4)
        return z >= row

    def to_chip(source, target, device, sem, half=None):
        arrival = half_sem.at[target] if half == 1 else recv_sem.at[target]
        return pltpu.make_async_remote_copy(
            src_ref=blocks.at[core, rows_of(source, half)],
            dst_ref=blocks.at[core, rows_of(target, half)],
            send_sem=send_sem.at[sem],
            recv_sem=arrival,
            device_id=device,
            device_id_type=pl.DeviceIdType.MESH,
        )

    def to_partner(slot):
        return pltpu.make_async_remote_copy(
            src_ref=blocks.at[core, rows_of(slot)],
            dst_ref=blocks.at[core, rows_of(slot)],
            send_sem=pair_send_sem.at[slot],
            recv_sem=pair_recv_sem.at[slot],
            device_id=partner,
            device_id_type=pl.DeviceIdType.MESH,
        )

    def from_partner(slot):
        return pltpu.make_async_remote_copy(
            src_ref=blocks.at[1 - core, rows_of(slot)],
            dst_ref=blocks.at[1 - core, rows_of(slot)],
            send_sem=pair_send_sem.at[slot],
            recv_sem=pair_recv_sem.at[slot],
            device_id=partner,
            device_id_type=pl.DeviceIdType.MESH,
        )

    sends = []

    def plan(source, target, device, half, condition):
        sends.append((source, target, device, half, condition))

    ahead = {1: x_next, 2: x_across, 3: x_last}
    below = z < Z_SIZE - 1
    for half in range(2):
        plan(OWN, SLOT[(1, 0)], z_next, half, below)
    for step in (1, 3, 2):
        plan(OWN, SLOT[(None, step)], ahead[step], None, x + step < X_SIZE)
    for row in (1, 2, 3):
        have = z >= row
        slot = SLOT[(row, 0)]
        for half in range(2):
            plan(slot, SLOT[(row + 1, 0)], z_next, half, jnp.logical_and(have, below))
            if (row, 1) not in ALONG_Z:
                plan(slot, SLOT[(row, 1)], x_next, half, have)
            if (row, 3) not in ALONG_Z:
                plan(slot, SLOT[(row, 3)], x_last, half, have)
            for step in (1, 2, 3):
                if (row + 1, step) in ALONG_Z:
                    target = SLOT[(row + 1, step)]
                    plan(SLOT[(row, step)], target, z_next, half, jnp.logical_and(have, below))
        if (row, 2) not in ALONG_Z:
            plan(SLOT[(row, 1)], SLOT[(row, 2)], x_next, 0, have)
            plan(SLOT[(row, 3)], SLOT[(row, 2)], x_last, 1, have)
    for step in (1, 3, 2):
        condition = jnp.logical_and(x + step >= X_SIZE, z >= 4)
        plan(SLOT[(4, 0)], SLOT[(None, step)], ahead[step], None, condition)

    def send_from(slot, halves):
        for sem, (source, target, device, half, condition) in enumerate(sends):
            if source == slot and half in halves:

                @pl.when(condition)
                def _():
                    to_chip(source, target, device, sem, half).start()

    def arrived(place, half=None):
        slot = SLOT[place]
        if place[0] is None:
            halves = (None,)
        elif half is None:
            halves = (0, 1)
        else:
            halves = (half,)

        @pl.when(holds(slot))
        def _():
            for part in halves:
                to_chip(slot, slot, x_next, 0, part).wait_recv()
            if halves[-1] != 0:
                to_partner(slot).start()

        send_from(slot, halves + (None,) if halves[-1] == 1 else halves)

    def wait_partner(slot):
        @pl.when(holds(slot))
        def _():
            from_partner(slot).wait_recv()

    fetch_own.wait()

    def prepare_keys(unit):
        @pl.when(core == 0)
        def _():
            rows = slice(unit * UNIT, (unit + 1) * UNIT)
            blocks[0, rows, :] = norm_rotate(
                blocks[0, rows, :], with_gain(unit, key_gain_ref), None
            )

    prepare_keys(0)
    for slot in range(1, SLOTS):

        @pl.when(jnp.logical_not(holds(slot)))
        def _():
            blocks[0, rows_of(slot), :] = jnp.zeros((SHARD, HD), jnp.bfloat16)

    pl.semaphore_wait(
        barrier, 4 + jnp.where(z > 0, 1, 0) + jnp.where(z < Z_SIZE - 1, 1, 0)
    )

    send_from(OWN, (0,))
    prepare_keys(1)
    send_from(OWN, (1,))
    to_partner(OWN).start()
    send_from(OWN, (None,))

    fetch_gain.wait()
    fetch_query.wait()

    def prepare_queries(unit):
        gained = with_gain(unit, query_gain_ref)
        for local in range(LOCAL_HEADS):
            rows = query_raw[
                unit * UNIT : (unit + 1) * UNIT, local * HD : (local + 1) * HD
            ]
            queries[unit, local * UNIT : (local + 1) * UNIT, :] = norm_rotate(
                rows, gained, HD**-0.5
            )

    def scores(unit, part, part_rows, keys):
        return lax.dot_general(
            queries[unit, part * part_rows : (part + 1) * part_rows, :],
            keys,
            (((1,), (1,)), ((), ())),
            preferred_element_type=jnp.float32,
        )

    def masked_values(values, allowed):
        zero = jnp.zeros_like(values)
        return jnp.concatenate(
            [jnp.where(allowed, values, zero), jnp.where(allowed, zero + 1, zero)], axis=1
        )

    own_first = ctx * UNITS

    def attend_own():
        keys = blocks[0, : UNITS * UNIT, :]
        row = lax.broadcasted_iota(jnp.int32, (SHARD, HD), 0) // UNIT
        unit_of_key = own_first + row
        shape = (UNIT, UNIT)
        causal = lax.broadcasted_iota(jnp.int32, shape, 1) <= lax.broadcasted_iota(
            jnp.int32, shape, 0
        )
        values = [
            masked_values(blocks[1, :SHARD, :], unit_of_key >= doc_units[unit])
            for unit in range(UNITS)
        ]
        parts = [(unit, part) for unit in range(UNITS) for part in range(LOCAL_HEADS)]

        def part_scores(unit, part):
            return scores(unit, part, UNIT, keys[: (unit + 1) * UNIT])

        held = part_scores(*parts[0])
        for index, (unit, part) in enumerate(parts):
            later = None
            if index + 1 < len(parts):
                later = part_scores(*parts[index + 1])
            weights = jnp.exp(held)
            corner_weights = jnp.where(causal, weights[:, unit * UNIT :], 0.0)
            if unit:
                weights = jnp.concatenate([weights[:, : unit * UNIT], corner_weights], axis=1)
            else:
                weights = corner_weights
            totals[unit, part * UNIT : (part + 1) * UNIT, :] = jnp.dot(
                weights.astype(jnp.bfloat16),
                values[unit][: (unit + 1) * UNIT],
                preferred_element_type=jnp.float32,
            )
            held = later

    prepare_queries(0)
    prepare_queries(1)
    from_partner(OWN).wait_recv()
    for arrival in EARLY:
        arrived(*arrival)
    attend_own()

    def attend(slot, width):
        count = width * SHARD
        at = pl.ds(pl.multiple_of(slot * SHARD, SHARD), count)
        keys = blocks[0, at, :]
        values = blocks[1, at, :]
        row = lax.broadcasted_iota(jnp.int32, (SHARD, HD), 0) // UNIT
        key_unit = jnp.concatenate(
            [row + first_units[slot + place] for place in range(width)], axis=0
        )
        masked = [masked_values(values, key_unit >= doc_units[unit]) for unit in range(UNITS)]
        part_rows = 512
        parts = [(unit, part) for unit in range(UNITS) for part in range(ROWS // part_rows)]
        held = scores(*parts[0], part_rows, keys)
        for index, (unit, part) in enumerate(parts):
            later = None
            if index + 1 < len(parts):
                later = scores(*parts[index + 1], part_rows, keys)
            weights = jnp.exp(held).astype(jnp.bfloat16)
            totals[unit, part * part_rows : (part + 1) * part_rows, :] += jnp.dot(
                weights, masked[unit], preferred_element_type=jnp.float32
            )
            held = later

    single_events = {
        1: [((3, 0), 0)],
        2: [((3, 0), 1)],
        3: [((1, 1), 0), ((1, 3), 0), ((1, 3), 1), ((1, 1), 1)],
        4: [((4, 0), 0), ((2, 1), 0), ((4, 0), 1)],
        5: [((2, 3), 0)],
        6: [((2, 3), 1), ((2, 1), 1)],
        7: [((1, 2), 0), ((3, 3), 0)],
        8: [((3, 1), 0), ((3, 3), 1), ((3, 1), 1), ((1, 2), 1)],
    }
    pair_events = {
        0: [((2, 2), 0), ((2, 2), 1)],
        1: [((None, 1),), ((3, 2), 0), ((3, 2), 1)],
        2: [((None, 3),), ((None, 2),)],
        3: [],
    }
    singles = len(single_events)

    def take(step, events, first, width):
        for index, arrivals in events.items():

            @pl.when(step == index)
            def _():
                for arrival in arrivals:
                    arrived(*arrival)
                for place in range(width):
                    wait_partner(first + width * index + place)

    def single(step, carry):
        take(step, single_events, 0, 1)
        attend(step, 1)
        return carry

    lax.fori_loop(1, 1 + singles, single, 0)

    def pair(step, carry):
        take(step, pair_events, 1 + singles, 2)
        attend(1 + singles + 2 * step, 2)
        return carry

    lax.fori_loop(0, len(pair_events), pair, 0)

    for unit in range(UNITS):
        for local in range(LOCAL_HEADS):
            rows = slice(local * UNIT, (local + 1) * UNIT)
            out_ref[unit * UNIT : (unit + 1) * UNIT, local * HD : (local + 1) * HD] = (
                totals[unit, rows, :HD] / totals[unit, rows, HD:]
            ).astype(jnp.bfloat16)

    for sem, (source, target, device, half, condition) in enumerate(sends):

        @pl.when(condition)
        def _():
            to_chip(source, target, device, sem, half).wait_send()

    for slot in range(SLOTS):

        @pl.when(holds(slot))
        def _():
            to_partner(slot).wait_send()


def per_device(query_proj, key_value, query_gain, key_gain, doc_offsets):
    row_table, base_table = rope_tables()
    return pl.pallas_call(
        attention_kernel,
        out_shape=jax.ShapeDtypeStruct((SHARD, LOCAL_HEADS * HD), jnp.bfloat16),
        in_specs=[pl.BlockSpec(memory_space=pltpu.HBM)] * 7,
        out_specs=pl.BlockSpec(memory_space=pltpu.VMEM),
        scratch_shapes=[
            pltpu.VMEM((SHARD, LOCAL_HEADS * HD), jnp.bfloat16),
            pltpu.VMEM((UNIT, 2 * HD), jnp.float32),
            pltpu.VMEM((HD,), jnp.float32),
            pltpu.VMEM((HD,), jnp.float32),
            pltpu.SMEM(doc_offsets.shape, jnp.int32),
            pltpu.VMEM((64, 2 * HD), jnp.float32),
            pltpu.VMEM((UNITS, ROWS, HD), jnp.bfloat16),
            pltpu.VMEM((2, SLOTS * SHARD, HD), jnp.bfloat16),
            pltpu.VMEM((UNITS, ROWS, 2 * HD), jnp.float32),
            pltpu.SMEM((SLOTS,), jnp.int32),
            pltpu.SemaphoreType.DMA((7,)),
            pltpu.SemaphoreType.DMA((40,)),
            pltpu.SemaphoreType.DMA((SLOTS,)),
            pltpu.SemaphoreType.DMA((SLOTS,)),
            pltpu.SemaphoreType.DMA((SLOTS,)),
            pltpu.SemaphoreType.DMA((SLOTS,)),
        ],
        compiler_params=pltpu.CompilerParams(
            collective_id=0, has_side_effects=True, vmem_limit_bytes=64 * 1024 * 1024
        ),
        cost_estimate=pl.CostEstimate(
            flops=2 * 2 * 2048 * 8448 * HD, bytes_accessed=2 << 20, transcendentals=2048 * 8448
        ),
    )(
        query_proj,
        key_value,
        jnp.asarray(row_table),
        query_gain,
        key_gain,
        doc_offsets,
        jnp.asarray(base_table),
    )


def solution(mesh):
    placed = (P("ctx", "head"), P("ctx", "head"), P(), P(), P())
    return jax.shard_map(
        per_device, mesh=mesh, in_specs=placed, out_specs=P("ctx", "head"), check_vma=False
    )
```

```python
import functools

import jax
import jax.numpy as jnp
import numpy as np
from jax import lax
from jax.experimental import pallas as pl
from jax.experimental.pallas import tpu as pltpu
from jax.sharding import PartitionSpec as P

HD = 128
UNIT = 256
SHARD = 512
UNITS = 2
LOCAL_HEADS = 4
ROWS = LOCAL_HEADS * UNIT
X_SIZE = 4
Z_SIZE = 8
NORM_EPS = 1e-06
ROPE_BASE = 1000000.0

OWN = 0
ORDER = [
    (0, 0),
    (1, 0),
    (2, 0),
    (1, 3),
    (3, 0),
    (1, 1),
    (4, 0),
    (2, 3),
    (3, 3),
    (1, 2),
    (2, 1),
    (None, 3),
    (2, 2),
    (3, 1),
    (None, 1),
    (3, 2),
    (None, 2),
]
EARLY = [((1, 0), 0), ((1, 0), 1)]
ALONG_Z = ((3, 1), (3, 3), (2, 2), (3, 2))
SLOT = {place: index for index, place in enumerate(ORDER)}
SLOTS = len(ORDER)
PARTS = 2


def rope_tables():
    frequency = ROPE_BASE ** (-np.arange(HD // 2, dtype=np.float64) * 2.0 / HD)
    sign = np.concatenate([-np.ones(HD // 2), np.ones(HD // 2)])

    def table(positions):
        angle = positions[:, None].astype(np.float64) * np.concatenate([frequency, frequency])
        return np.concatenate([np.cos(angle), np.sin(angle) * sign], axis=1).astype(np.float32)

    return table(np.arange(UNIT)), table(np.arange(64) * UNIT)


def attention_kernel(
    query_hbm,
    key_value_hbm,
    row_table_hbm,
    query_gain_hbm,
    key_gain_hbm,
    offsets_hbm,
    base_table_hbm,
    out_ref,
    query_raw,
    row_table,
    query_gain_ref,
    key_gain_ref,
    offsets_ref,
    base_table_ref,
    queries,
    blocks,
    totals,
    first_units,
    local_sem,
    send_sem,
    recv_sem,
    pair_send_sem,
    pair_recv_sem,
):
    ctx = lax.axis_index("ctx")
    head = lax.axis_index("head")
    z, x = ctx // X_SIZE, ctx % X_SIZE
    core = head % 2

    def place(z_to, x_to):
        return (((z_to + Z_SIZE) % Z_SIZE) * X_SIZE + (x_to + X_SIZE) % X_SIZE, head)

    z_next, z_last = place(z + 1, x), place(z - 1, x)
    x_next, x_last, x_across = place(z, x + 1), place(z, x - 1), place(z, x + 2)
    partner = (ctx, head + 1 - 2 * core)

    barrier = pltpu.get_barrier_semaphore()

    def greet(other):
        pl.semaphore_signal(barrier, inc=1, device_id=other, device_id_type=pl.DeviceIdType.MESH)

    @pl.when(z > 0)
    def _():
        greet(z_last)

    @pl.when(z < Z_SIZE - 1)
    def _():
        greet(z_next)

    for other in (x_next, x_last, x_across, partner):
        greet(other)

    own_rows = pl.ds(0, SHARD)
    fetches = [
        pltpu.make_async_copy(source, target, local_sem.at[index])
        for index, (source, target) in enumerate(
            (
                (offsets_hbm, offsets_ref),
                (base_table_hbm, base_table_ref),
                (key_gain_hbm, key_gain_ref),
                (key_value_hbm, blocks.at[core, own_rows]),
                (row_table_hbm, row_table),
                (query_gain_hbm, query_gain_ref),
                (query_hbm, query_raw),
            )
        )
    ]
    for fetch in fetches:
        fetch.start()
    fetch_offsets, fetch_base, fetch_key_gain, fetch_own, fetch_table, fetch_gain, fetch_query = fetches

    fetch_offsets.wait()
    doc_units = []
    for unit in range(UNITS):
        first = (ctx * UNITS + unit) * UNIT
        start = 0
        for entry in range(offsets_ref.shape[0]):
            offset = offsets_ref[entry]
            start = jnp.maximum(start, jnp.where(offset <= first, offset, 0))
        doc_units.append(start // UNIT)

    for index, (row, step) in enumerate(ORDER):
        if row is None:
            shard = jnp.where(x >= step, ctx - step, ctx - 4 * X_SIZE - step + X_SIZE)
        else:
            shard = ctx - row * X_SIZE - step + jnp.where(x >= step, 0, X_SIZE)
        first_units[index] = shard * UNITS

    fetch_base.wait()
    fetch_key_gain.wait()
    fetch_table.wait()

    def unit_tables(unit):
        behind = ctx * UNITS + unit - doc_units[unit]
        base = base_table_ref[pl.ds(behind, 1), :]
        base_cos, base_sin = base[:, :HD], base[:, HD:]
        row_cos, row_sin = row_table[:, :HD], row_table[:, HD:]
        cosines = base_cos * row_cos - base_sin * row_sin
        sines = base_sin * row_cos + base_cos * row_sin
        return cosines, sines

    tables = [unit_tables(unit) for unit in range(UNITS)]

    def with_gain(unit, gain_ref):
        gain = gain_ref[...].reshape(1, HD)
        cosines, sines = tables[unit]
        return cosines * gain, sines * pltpu.roll(gain, HD // 2, 1)

    def norm_rotate(rows, gained, scale):
        wide = rows.astype(jnp.float32)
        mean_square = jnp.mean(wide * wide, axis=1, keepdims=True)
        factor = lax.rsqrt(mean_square + NORM_EPS)
        if scale is not None:
            factor = factor * scale
        turned = wide * gained[0] + pltpu.roll(wide, HD // 2, 1) * gained[1]
        return (turned * factor).astype(jnp.bfloat16)

    def rows_of(slot, part=None):
        if part is None:
            return pl.ds(slot * SHARD, SHARD)
        return pl.ds(slot * SHARD + part * (SHARD // PARTS), SHARD // PARTS)

    def holds(slot):
        row, step = ORDER[slot]
        if row is None:
            return jnp.logical_or(x >= step, z >= 4)
        return z >= row

    def to_chip(source, target, device, sem, part=None):
        return pltpu.make_async_remote_copy(
            src_ref=blocks.at[core, rows_of(source, part)],
            dst_ref=blocks.at[core, rows_of(target, part)],
            send_sem=send_sem.at[sem],
            recv_sem=recv_sem.at[target * PARTS + (part or 0)],
            device_id=device,
            device_id_type=pl.DeviceIdType.MESH,
        )

    def to_partner(slot):
        return pltpu.make_async_remote_copy(
            src_ref=blocks.at[core, rows_of(slot)],
            dst_ref=blocks.at[core, rows_of(slot)],
            send_sem=pair_send_sem.at[slot],
            recv_sem=pair_recv_sem.at[slot],
            device_id=partner,
            device_id_type=pl.DeviceIdType.MESH,
        )

    def from_partner(slot):
        return pltpu.make_async_remote_copy(
            src_ref=blocks.at[1 - core, rows_of(slot)],
            dst_ref=blocks.at[1 - core, rows_of(slot)],
            send_sem=pair_send_sem.at[slot],
            recv_sem=pair_recv_sem.at[slot],
            device_id=partner,
            device_id_type=pl.DeviceIdType.MESH,
        )

    sends = []

    def plan(source, target, device, part, condition):
        sends.append((source, target, device, part, condition))

    ahead = {1: x_next, 2: x_across, 3: x_last}
    below = z < Z_SIZE - 1
    for part in range(PARTS):
        plan(OWN, SLOT[(1, 0)], z_next, part, below)
    for step in (1, 3, 2):
        plan(OWN, SLOT[(None, step)], ahead[step], None, x + step < X_SIZE)
    for row in (1, 2, 3):
        have = z >= row
        slot = SLOT[(row, 0)]
        for part in range(PARTS):
            plan(slot, SLOT[(row + 1, 0)], z_next, part, jnp.logical_and(have, below))
            if (row, 1) not in ALONG_Z:
                plan(slot, SLOT[(row, 1)], x_next, part, have)
            if (row, 3) not in ALONG_Z:
                plan(slot, SLOT[(row, 3)], x_last, part, have)
            for step in (1, 2, 3):
                if (row + 1, step) in ALONG_Z:
                    target = SLOT[(row + 1, step)]
                    plan(SLOT[(row, step)], target, z_next, part, jnp.logical_and(have, below))
            if (row, 2) not in ALONG_Z:
                if part < PARTS // 2:
                    plan(SLOT[(row, 1)], SLOT[(row, 2)], x_next, part, have)
                else:
                    plan(SLOT[(row, 3)], SLOT[(row, 2)], x_last, part, have)
    for step in (1, 3, 2):
        condition = jnp.logical_and(x + step >= X_SIZE, z >= 4)
        plan(SLOT[(4, 0)], SLOT[(None, step)], ahead[step], None, condition)

    def send_from(slot, parts):
        for sem, (source, target, device, part, condition) in enumerate(sends):
            if source == slot and part in parts:

                @pl.when(condition)
                def _():
                    to_chip(source, target, device, sem, part).start()

    def arrived(place, half=None):
        slot = SLOT[place]
        if place[0] is None:
            parts = (None,)
        else:
            parts = tuple(range(half * PARTS // 2, (half + 1) * PARTS // 2))
        whole = parts[-1] in (None, PARTS - 1)

        for part in parts:

            @pl.when(holds(slot))
            def _():
                to_chip(slot, slot, x_next, 0, part).wait_recv()

            if part == parts[-1] and whole:

                @pl.when(holds(slot))
                def _():
                    to_partner(slot).start()

            if part is not None:
                send_from(slot, (part,))
        if whole and place[0] is not None:
            send_from(slot, (None,))

    def wait_partner(slot):
        @pl.when(holds(slot))
        def _():
            from_partner(slot).wait_recv()

    fetch_own.wait()

    def prepare_keys(unit):
        @pl.when(core == 0)
        def _():
            rows = slice(unit * UNIT, (unit + 1) * UNIT)
            blocks[0, rows, :] = norm_rotate(
                blocks[0, rows, :], with_gain(unit, key_gain_ref), None
            )

    prepare_keys(0)
    for slot in range(1, SLOTS):

        @pl.when(jnp.logical_not(holds(slot)))
        def _():
            blocks[0, rows_of(slot), :] = jnp.zeros((SHARD, HD), jnp.bfloat16)

    pl.semaphore_wait(
        barrier, 4 + jnp.where(z > 0, 1, 0) + jnp.where(z < Z_SIZE - 1, 1, 0)
    )

    send_from(OWN, tuple(range(PARTS // 2)))
    prepare_keys(1)
    send_from(OWN, tuple(range(PARTS // 2, PARTS)))
    to_partner(OWN).start()
    send_from(OWN, (None,))

    fetch_gain.wait()
    fetch_query.wait()

    def prepare_queries(unit):
        gained = with_gain(unit, query_gain_ref)
        for local in range(LOCAL_HEADS):
            rows = query_raw[
                unit * UNIT : (unit + 1) * UNIT, local * HD : (local + 1) * HD
            ]
            queries[unit, local * UNIT : (local + 1) * UNIT, :] = norm_rotate(
                rows, gained, HD**-0.5
            )

    def scores(unit, part, part_rows, keys):
        return lax.dot_general(
            queries[unit, part * part_rows : (part + 1) * part_rows, :],
            keys,
            (((1,), (1,)), ((), ())),
            preferred_element_type=jnp.float32,
        )

    def masked_values(values, allowed):
        zero = jnp.zeros_like(values)
        return jnp.concatenate(
            [jnp.where(allowed, values, zero), jnp.where(allowed, zero + 1, zero)], axis=1
        )

    own_first = ctx * UNITS

    def attend_own():
        keys = blocks[0, : UNITS * UNIT, :]
        row = lax.broadcasted_iota(jnp.int32, (SHARD, HD), 0) // UNIT
        unit_of_key = own_first + row
        shape = (UNIT, UNIT)
        causal = lax.broadcasted_iota(jnp.int32, shape, 1) <= lax.broadcasted_iota(
            jnp.int32, shape, 0
        )
        values = [
            masked_values(blocks[1, :SHARD, :], unit_of_key >= doc_units[unit])
            for unit in range(UNITS)
        ]
        parts = [(unit, part) for unit in range(UNITS) for part in range(LOCAL_HEADS)]

        def part_scores(unit, part):
            return scores(unit, part, UNIT, keys[: (unit + 1) * UNIT])

        held = part_scores(*parts[0])
        for index, (unit, part) in enumerate(parts):
            later = None
            if index + 1 < len(parts):
                later = part_scores(*parts[index + 1])
            weights = jnp.exp(held)
            corner_weights = jnp.where(causal, weights[:, unit * UNIT :], 0.0)
            if unit:
                weights = jnp.concatenate([weights[:, : unit * UNIT], corner_weights], axis=1)
            else:
                weights = corner_weights
            totals[unit, part * UNIT : (part + 1) * UNIT, :] = jnp.dot(
                weights.astype(jnp.bfloat16),
                values[unit][: (unit + 1) * UNIT],
                preferred_element_type=jnp.float32,
            )
            held = later

    prepare_queries(0)
    prepare_queries(1)
    from_partner(OWN).wait_recv()
    for arrival in EARLY:
        arrived(*arrival)
    attend_own()

    def attend(slot, width):
        count = width * SHARD
        at = pl.ds(pl.multiple_of(slot * SHARD, SHARD), count)
        keys = blocks[0, at, :]
        values = blocks[1, at, :]
        row = lax.broadcasted_iota(jnp.int32, (SHARD, HD), 0) // UNIT
        key_unit = jnp.concatenate(
            [row + first_units[slot + place] for place in range(width)], axis=0
        )
        masked = [masked_values(values, key_unit >= doc_units[unit]) for unit in range(UNITS)]
        part_rows = 512
        parts = [(unit, part) for unit in range(UNITS) for part in range(ROWS // part_rows)]
        held = scores(*parts[0], part_rows, keys)
        for index, (unit, part) in enumerate(parts):
            later = None
            if index + 1 < len(parts):
                later = scores(*parts[index + 1], part_rows, keys)
            weights = jnp.exp(held).astype(jnp.bfloat16)
            totals[unit, part * part_rows : (part + 1) * part_rows, :] += jnp.dot(
                weights, masked[unit], preferred_element_type=jnp.float32
            )
            held = later

    single_events = {
        1: [((2, 0), 0), ((2, 0), 1)],
        2: [((1, 3), 0), ((3, 0), 0), ((1, 3), 1), ((3, 0), 1), ((1, 1), 0)],
        3: [((1, 1), 1), ((4, 0), 0), ((2, 3), 0)],
        4: [((4, 0), 1), ((2, 1), 0)],
        5: [((2, 3), 1)],
        6: [((1, 2), 0), ((1, 2), 1)],
        7: [((3, 3), 0), ((3, 1), 0), ((2, 1), 1), ((3, 3), 1)],
        8: [((2, 2), 0)],
    }
    pair_events = {
        0: [((2, 2), 1), ((None, 3),)],
        1: [((None, 2),), ((3, 1), 1), ((None, 1),), ((3, 2), 0)],
        2: [((3, 2), 1)],
        3: [],
    }
    singles = len(single_events)

    def take(step, events, first, width):
        for index, arrivals in events.items():

            @pl.when(step == index)
            def _():
                for arrival in arrivals:
                    arrived(*arrival)
                for place in range(width):
                    wait_partner(first + width * index + place)

    def needed(step, events, first, width):
        found = False
        for index in events:
            slots = [first + width * index + place for place in range(width)]
            exists = functools.reduce(jnp.logical_or, [holds(slot) for slot in slots])
            found = jnp.logical_or(found, jnp.logical_and(step == index, exists))
        return found

    def single(step, carry):
        take(step, single_events, 0, 1)

        @pl.when(needed(step, single_events, 0, 1))
        def _():
            attend(step, 1)

        return carry

    lax.fori_loop(1, 1 + singles, single, 0)

    def pair(step, carry):
        take(step, pair_events, 1 + singles, 2)

        @pl.when(needed(step, pair_events, 1 + singles, 2))
        def _():
            attend(1 + singles + 2 * step, 2)

        return carry

    lax.fori_loop(0, len(pair_events), pair, 0)

    for unit in range(UNITS):
        for local in range(LOCAL_HEADS):
            rows = slice(local * UNIT, (local + 1) * UNIT)
            out_ref[unit * UNIT : (unit + 1) * UNIT, local * HD : (local + 1) * HD] = (
                totals[unit, rows, :HD] / totals[unit, rows, HD:]
            ).astype(jnp.bfloat16)

    for sem, (source, target, device, part, condition) in enumerate(sends):

        @pl.when(condition)
        def _():
            to_chip(source, target, device, sem, part).wait_send()

    for slot in range(SLOTS):

        @pl.when(holds(slot))
        def _():
            to_partner(slot).wait_send()


def per_device(query_proj, key_value, query_gain, key_gain, doc_offsets):
    row_table, base_table = rope_tables()
    return pl.pallas_call(
        attention_kernel,
        out_shape=jax.ShapeDtypeStruct((SHARD, LOCAL_HEADS * HD), jnp.bfloat16),
        in_specs=[pl.BlockSpec(memory_space=pltpu.HBM)] * 7,
        out_specs=pl.BlockSpec(memory_space=pltpu.VMEM),
        scratch_shapes=[
            pltpu.VMEM((SHARD, LOCAL_HEADS * HD), jnp.bfloat16),
            pltpu.VMEM((UNIT, 2 * HD), jnp.float32),
            pltpu.VMEM((HD,), jnp.float32),
            pltpu.VMEM((HD,), jnp.float32),
            pltpu.SMEM(doc_offsets.shape, jnp.int32),
            pltpu.VMEM((64, 2 * HD), jnp.float32),
            pltpu.VMEM((UNITS, ROWS, HD), jnp.bfloat16),
            pltpu.VMEM((2, SLOTS * SHARD, HD), jnp.bfloat16),
            pltpu.VMEM((UNITS, ROWS, 2 * HD), jnp.float32),
            pltpu.SMEM((SLOTS,), jnp.int32),
            pltpu.SemaphoreType.DMA((7,)),
            pltpu.SemaphoreType.DMA((96,)),
            pltpu.SemaphoreType.DMA((SLOTS * PARTS,)),
            pltpu.SemaphoreType.DMA((SLOTS,)),
            pltpu.SemaphoreType.DMA((SLOTS,)),
        ],
        compiler_params=pltpu.CompilerParams(
            collective_id=0, has_side_effects=True, vmem_limit_bytes=64 * 1024 * 1024
        ),
        cost_estimate=pl.CostEstimate(
            flops=2 * 2 * 2048 * 8448 * HD, bytes_accessed=2 << 20, transcendentals=2048 * 8448
        ),
    )(
        query_proj,
        key_value,
        jnp.asarray(row_table),
        query_gain,
        key_gain,
        doc_offsets,
        jnp.asarray(base_table),
    )


def solution(mesh):
    placed = (P("ctx", "head"), P("ctx", "head"), P(), P(), P())
    return jax.shard_map(
        per_device, mesh=mesh, in_specs=placed, out_specs=P("ctx", "head"), check_vma=False
    )
```

```python
import functools

import jax
import jax.numpy as jnp
import numpy as np
from jax import lax
from jax.experimental import pallas as pl
from jax.experimental.pallas import tpu as pltpu
from jax.sharding import PartitionSpec as P

HD = 128
UNIT = 256
SHARD = 512
UNITS = 2
LOCAL_HEADS = 4
ROWS = LOCAL_HEADS * UNIT
X_SIZE = 4
Z_SIZE = 8
NORM_EPS = 1e-06
ROPE_BASE = 1000000.0

OWN = 0
ORDER = [
    (0, 0),
    (1, 0),
    (2, 0),
    (1, 3),
    (3, 0),
    (1, 1),
    (4, 0),
    (2, 3),
    (3, 3),
    (1, 2),
    (2, 1),
    (None, 3),
    (2, 2),
    (3, 1),
    (None, 1),
    (3, 2),
    (None, 2),
]
EARLY = [((1, 0), 0), ((1, 0), 1)]
ALONG_Z = ((3, 1), (3, 3), (2, 2), (3, 2))
SLOT = {place: index for index, place in enumerate(ORDER)}
SLOTS = len(ORDER)
PARTS = 2


def rope_tables():
    frequency = ROPE_BASE ** (-np.arange(HD // 2, dtype=np.float64) * 2.0 / HD)
    sign = np.concatenate([-np.ones(HD // 2), np.ones(HD // 2)])

    def table(positions):
        angle = positions[:, None].astype(np.float64) * np.concatenate([frequency, frequency])
        return np.concatenate([np.cos(angle), np.sin(angle) * sign], axis=1).astype(np.float32)

    return table(np.arange(UNIT)), table(np.arange(64) * UNIT)


def attention_kernel(
    query_hbm,
    key_value_hbm,
    row_table_hbm,
    query_gain_hbm,
    key_gain_hbm,
    offsets_hbm,
    base_table_hbm,
    out_ref,
    query_raw,
    row_table,
    query_gain_ref,
    key_gain_ref,
    offsets_ref,
    base_table_ref,
    queries,
    blocks,
    totals,
    first_units,
    local_sem,
    send_sem,
    recv_sem,
    pair_send_sem,
    pair_recv_sem,
):
    ctx = lax.axis_index("ctx")
    head = lax.axis_index("head")
    z, x = ctx // X_SIZE, ctx % X_SIZE
    core = head % 2

    def place(z_to, x_to):
        return (((z_to + Z_SIZE) % Z_SIZE) * X_SIZE + (x_to + X_SIZE) % X_SIZE, head)

    z_next, z_last = place(z + 1, x), place(z - 1, x)
    x_next, x_last, x_across = place(z, x + 1), place(z, x - 1), place(z, x + 2)
    partner = (ctx, head + 1 - 2 * core)

    barrier = pltpu.get_barrier_semaphore()

    def greet(other):
        pl.semaphore_signal(barrier, inc=1, device_id=other, device_id_type=pl.DeviceIdType.MESH)

    @pl.when(z > 0)
    def _():
        greet(z_last)

    @pl.when(z < Z_SIZE - 1)
    def _():
        greet(z_next)

    for other in (x_next, x_last, x_across, partner):
        greet(other)

    own_rows = pl.ds(0, SHARD)
    fetches = [
        pltpu.make_async_copy(source, target, local_sem.at[index])
        for index, (source, target) in enumerate(
            (
                (offsets_hbm, offsets_ref),
                (base_table_hbm, base_table_ref),
                (key_gain_hbm, key_gain_ref),
                (key_value_hbm, blocks.at[core, own_rows]),
                (row_table_hbm, row_table),
                (query_gain_hbm, query_gain_ref),
                (query_hbm, query_raw),
            )
        )
    ]
    for fetch in fetches:
        fetch.start()
    fetch_offsets, fetch_base, fetch_key_gain, fetch_own, fetch_table, fetch_gain, fetch_query = fetches

    fetch_offsets.wait()
    doc_units = []
    for unit in range(UNITS):
        first = (ctx * UNITS + unit) * UNIT
        start = 0
        for entry in range(offsets_ref.shape[0]):
            offset = offsets_ref[entry]
            start = jnp.maximum(start, jnp.where(offset <= first, offset, 0))
        doc_units.append(start // UNIT)

    for index, (row, step) in enumerate(ORDER):
        if row is None:
            shard = jnp.where(x >= step, ctx - step, ctx - 4 * X_SIZE - step + X_SIZE)
        else:
            shard = ctx - row * X_SIZE - step + jnp.where(x >= step, 0, X_SIZE)
        first_units[index] = shard * UNITS

    fetch_base.wait()
    fetch_key_gain.wait()
    fetch_table.wait()

    def unit_tables(unit):
        behind = ctx * UNITS + unit - doc_units[unit]
        base = base_table_ref[pl.ds(behind, 1), :]
        base_cos, base_sin = base[:, :HD], base[:, HD:]
        row_cos, row_sin = row_table[:, :HD], row_table[:, HD:]
        cosines = base_cos * row_cos - base_sin * row_sin
        sines = base_sin * row_cos + base_cos * row_sin
        return cosines, sines

    tables = [unit_tables(unit) for unit in range(UNITS)]

    def with_gain(unit, gain_ref):
        gain = gain_ref[...].reshape(1, HD)
        cosines, sines = tables[unit]
        return cosines * gain, sines * pltpu.roll(gain, HD // 2, 1)

    def norm_rotate(rows, gained, scale):
        wide = rows.astype(jnp.float32)
        mean_square = jnp.mean(wide * wide, axis=1, keepdims=True)
        factor = lax.rsqrt(mean_square + NORM_EPS)
        if scale is not None:
            factor = factor * scale
        turned = wide * gained[0] + pltpu.roll(wide, HD // 2, 1) * gained[1]
        return (turned * factor).astype(jnp.bfloat16)

    def rows_of(slot, part=None):
        if part is None:
            return pl.ds(slot * SHARD, SHARD)
        return pl.ds(slot * SHARD + part * (SHARD // PARTS), SHARD // PARTS)

    def holds(slot):
        row, step = ORDER[slot]
        if row is None:
            return jnp.logical_or(x >= step, z >= 4)
        return z >= row

    def to_chip(source, target, device, sem, part=None):
        return pltpu.make_async_remote_copy(
            src_ref=blocks.at[core, rows_of(source, part)],
            dst_ref=blocks.at[core, rows_of(target, part)],
            send_sem=send_sem.at[sem],
            recv_sem=recv_sem.at[target * PARTS + (part or 0)],
            device_id=device,
            device_id_type=pl.DeviceIdType.MESH,
        )

    def to_partner(slot):
        return pltpu.make_async_remote_copy(
            src_ref=blocks.at[core, rows_of(slot)],
            dst_ref=blocks.at[core, rows_of(slot)],
            send_sem=pair_send_sem.at[slot],
            recv_sem=pair_recv_sem.at[slot],
            device_id=partner,
            device_id_type=pl.DeviceIdType.MESH,
        )

    def from_partner(slot):
        return pltpu.make_async_remote_copy(
            src_ref=blocks.at[1 - core, rows_of(slot)],
            dst_ref=blocks.at[1 - core, rows_of(slot)],
            send_sem=pair_send_sem.at[slot],
            recv_sem=pair_recv_sem.at[slot],
            device_id=partner,
            device_id_type=pl.DeviceIdType.MESH,
        )

    sends = []

    def plan(source, target, device, part, condition):
        sends.append((source, target, device, part, condition))

    ahead = {1: x_next, 2: x_across, 3: x_last}
    below = z < Z_SIZE - 1
    for part in range(PARTS):
        plan(OWN, SLOT[(1, 0)], z_next, part, below)
    for step in (1, 3, 2):
        plan(OWN, SLOT[(None, step)], ahead[step], None, x + step < X_SIZE)
    for row in (1, 2, 3):
        have = z >= row
        slot = SLOT[(row, 0)]
        for part in range(PARTS):
            plan(slot, SLOT[(row + 1, 0)], z_next, part, jnp.logical_and(have, below))
            if (row, 1) not in ALONG_Z:
                plan(slot, SLOT[(row, 1)], x_next, part, have)
            if (row, 3) not in ALONG_Z:
                plan(slot, SLOT[(row, 3)], x_last, part, have)
            for step in (1, 2, 3):
                if (row + 1, step) in ALONG_Z:
                    target = SLOT[(row + 1, step)]
                    plan(SLOT[(row, step)], target, z_next, part, jnp.logical_and(have, below))
            if (row, 2) not in ALONG_Z:
                if part < PARTS // 2:
                    plan(SLOT[(row, 1)], SLOT[(row, 2)], x_next, part, have)
                else:
                    plan(SLOT[(row, 3)], SLOT[(row, 2)], x_last, part, have)
    for step in (1, 3, 2):
        condition = jnp.logical_and(x + step >= X_SIZE, z >= 4)
        plan(SLOT[(4, 0)], SLOT[(None, step)], ahead[step], None, condition)

    def send_from(slot, parts):
        for sem, (source, target, device, part, condition) in enumerate(sends):
            if source == slot and part in parts:

                @pl.when(condition)
                def _():
                    to_chip(source, target, device, sem, part).start()

    def arrived(place, half=None):
        slot = SLOT[place]
        if place[0] is None:
            parts = (None,)
        else:
            parts = tuple(range(half * PARTS // 2, (half + 1) * PARTS // 2))
        whole = parts[-1] in (None, PARTS - 1)

        for part in parts:

            @pl.when(holds(slot))
            def _():
                to_chip(slot, slot, x_next, 0, part).wait_recv()

            if part == parts[-1] and whole:

                @pl.when(holds(slot))
                def _():
                    to_partner(slot).start()

            if part is not None:
                send_from(slot, (part,))
        if whole and place[0] is not None:
            send_from(slot, (None,))

    def wait_partner(slot):
        @pl.when(holds(slot))
        def _():
            from_partner(slot).wait_recv()

    fetch_own.wait()

    def prepare_keys(unit):
        @pl.when(core == 0)
        def _():
            rows = slice(unit * UNIT, (unit + 1) * UNIT)
            blocks[0, rows, :] = norm_rotate(
                blocks[0, rows, :], with_gain(unit, key_gain_ref), None
            )

    prepare_keys(0)
    for slot in range(1, SLOTS):

        @pl.when(jnp.logical_not(holds(slot)))
        def _():
            blocks[0, rows_of(slot), :] = jnp.zeros((SHARD, HD), jnp.bfloat16)

    pl.semaphore_wait(
        barrier, 4 + jnp.where(z > 0, 1, 0) + jnp.where(z < Z_SIZE - 1, 1, 0)
    )

    send_from(OWN, tuple(range(PARTS // 2)))
    prepare_keys(1)
    send_from(OWN, tuple(range(PARTS // 2, PARTS)))
    to_partner(OWN).start()
    send_from(OWN, (None,))

    fetch_gain.wait()
    fetch_query.wait()

    def prepare_queries(unit):
        gained = with_gain(unit, query_gain_ref)
        for local in range(LOCAL_HEADS):
            rows = query_raw[
                unit * UNIT : (unit + 1) * UNIT, local * HD : (local + 1) * HD
            ]
            queries[unit, local * UNIT : (local + 1) * UNIT, :] = norm_rotate(
                rows, gained, HD**-0.5
            )

    def scores(unit, part, part_rows, keys):
        return lax.dot_general(
            queries[unit, part * part_rows : (part + 1) * part_rows, :],
            keys,
            (((1,), (1,)), ((), ())),
            preferred_element_type=jnp.float32,
        )

    def masked_values(values, allowed):
        zero = jnp.zeros_like(values)
        return jnp.concatenate(
            [jnp.where(allowed, values, zero), jnp.where(allowed, zero + 1, zero)], axis=1
        )

    own_first = ctx * UNITS

    def attend_own(own_unit):
        keys = blocks[0, : UNITS * UNIT, :]
        row = lax.broadcasted_iota(jnp.int32, (SHARD, HD), 0) // UNIT
        unit_of_key = own_first + row
        shape = (UNIT, UNIT)
        causal = lax.broadcasted_iota(jnp.int32, shape, 1) <= lax.broadcasted_iota(
            jnp.int32, shape, 0
        )
        values = [
            masked_values(blocks[1, :SHARD, :], unit_of_key >= doc_units[unit])
            for unit in range(UNITS)
        ]
        parts = [(own_unit, part) for part in range(LOCAL_HEADS)]

        def part_scores(unit, part):
            return scores(unit, part, UNIT, keys[: (unit + 1) * UNIT])

        held = part_scores(*parts[0])
        for index, (unit, part) in enumerate(parts):
            later = None
            if index + 1 < len(parts):
                later = part_scores(*parts[index + 1])
            weights = jnp.exp(held)
            corner_weights = jnp.where(causal, weights[:, unit * UNIT :], 0.0)
            if unit:
                weights = jnp.concatenate([weights[:, : unit * UNIT], corner_weights], axis=1)
            else:
                weights = corner_weights
            totals[unit, part * UNIT : (part + 1) * UNIT, :] = jnp.dot(
                weights.astype(jnp.bfloat16),
                values[unit][: (unit + 1) * UNIT],
                preferred_element_type=jnp.float32,
            )
            held = later

    prepare_queries(0)
    prepare_queries(1)
    from_partner(OWN).wait_recv()
    for unit, arrival in enumerate(EARLY):
        attend_own(unit)
        arrived(*arrival)

    def attend(slot, width):
        count = width * SHARD
        at = pl.ds(pl.multiple_of(slot * SHARD, SHARD), count)
        keys = blocks[0, at, :]
        values = blocks[1, at, :]
        row = lax.broadcasted_iota(jnp.int32, (SHARD, HD), 0) // UNIT
        key_unit = jnp.concatenate(
            [row + first_units[slot + place] for place in range(width)], axis=0
        )
        masked = [masked_values(values, key_unit >= doc_units[unit]) for unit in range(UNITS)]
        part_rows = 512
        parts = [(unit, part) for unit in range(UNITS) for part in range(ROWS // part_rows)]
        held = scores(*parts[0], part_rows, keys)
        for index, (unit, part) in enumerate(parts):
            later = None
            if index + 1 < len(parts):
                later = scores(*parts[index + 1], part_rows, keys)
            weights = jnp.exp(held).astype(jnp.bfloat16)
            totals[unit, part * part_rows : (part + 1) * part_rows, :] += jnp.dot(
                weights, masked[unit], preferred_element_type=jnp.float32
            )
            held = later

    single_events = {
        1: [],
        2: [((2, 0), 0), ((2, 0), 1), ((1, 3), 0)],
        3: [((3, 0), 0), ((1, 3), 1), ((3, 0), 1), ((1, 1), 0), ((1, 1), 1), ((4, 0), 0), ((2, 3), 0)],
        4: [((4, 0), 1), ((2, 1), 0)],
        5: [((2, 3), 1)],
        6: [((1, 2), 0), ((1, 2), 1)],
        7: [((3, 3), 0), ((3, 1), 0), ((2, 1), 1), ((3, 3), 1)],
        8: [((2, 2), 0)],
    }
    pair_events = {
        0: [((2, 2), 1), ((None, 3),)],
        1: [((None, 2),), ((3, 1), 1), ((None, 1),), ((3, 2), 0)],
        2: [((3, 2), 1)],
        3: [],
    }
    singles = len(single_events)

    def take(step, events, first, width):
        for index, arrivals in events.items():

            @pl.when(step == index)
            def _():
                for arrival in arrivals:
                    arrived(*arrival)
                for place in range(width):
                    wait_partner(first + width * index + place)

    def needed(step, events, first, width):
        found = False
        for index in events:
            slots = [first + width * index + place for place in range(width)]
            exists = functools.reduce(jnp.logical_or, [holds(slot) for slot in slots])
            found = jnp.logical_or(found, jnp.logical_and(step == index, exists))
        return found

    def single(step, carry):
        take(step, single_events, 0, 1)

        @pl.when(needed(step, single_events, 0, 1))
        def _():
            attend(step, 1)

        return carry

    lax.fori_loop(1, 1 + singles, single, 0)

    def pair(step, carry):
        take(step, pair_events, 1 + singles, 2)

        @pl.when(needed(step, pair_events, 1 + singles, 2))
        def _():
            attend(1 + singles + 2 * step, 2)

        return carry

    lax.fori_loop(0, len(pair_events), pair, 0)

    for unit in range(UNITS):
        for local in range(LOCAL_HEADS):
            rows = slice(local * UNIT, (local + 1) * UNIT)
            out_ref[unit * UNIT : (unit + 1) * UNIT, local * HD : (local + 1) * HD] = (
                totals[unit, rows, :HD] / totals[unit, rows, HD:]
            ).astype(jnp.bfloat16)

    for sem, (source, target, device, part, condition) in enumerate(sends):

        @pl.when(condition)
        def _():
            to_chip(source, target, device, sem, part).wait_send()

    for slot in range(SLOTS):

        @pl.when(holds(slot))
        def _():
            to_partner(slot).wait_send()


def per_device(query_proj, key_value, query_gain, key_gain, doc_offsets):
    row_table, base_table = rope_tables()
    return pl.pallas_call(
        attention_kernel,
        out_shape=jax.ShapeDtypeStruct((SHARD, LOCAL_HEADS * HD), jnp.bfloat16),
        in_specs=[pl.BlockSpec(memory_space=pltpu.HBM)] * 7,
        out_specs=pl.BlockSpec(memory_space=pltpu.VMEM),
        scratch_shapes=[
            pltpu.VMEM((SHARD, LOCAL_HEADS * HD), jnp.bfloat16),
            pltpu.VMEM((UNIT, 2 * HD), jnp.float32),
            pltpu.VMEM((HD,), jnp.float32),
            pltpu.VMEM((HD,), jnp.float32),
            pltpu.SMEM(doc_offsets.shape, jnp.int32),
            pltpu.VMEM((64, 2 * HD), jnp.float32),
            pltpu.VMEM((UNITS, ROWS, HD), jnp.bfloat16),
            pltpu.VMEM((2, SLOTS * SHARD, HD), jnp.bfloat16),
            pltpu.VMEM((UNITS, ROWS, 2 * HD), jnp.float32),
            pltpu.SMEM((SLOTS,), jnp.int32),
            pltpu.SemaphoreType.DMA((7,)),
            pltpu.SemaphoreType.DMA((96,)),
            pltpu.SemaphoreType.DMA((SLOTS * PARTS,)),
            pltpu.SemaphoreType.DMA((SLOTS,)),
            pltpu.SemaphoreType.DMA((SLOTS,)),
        ],
        compiler_params=pltpu.CompilerParams(
            collective_id=0, has_side_effects=True, vmem_limit_bytes=64 * 1024 * 1024
        ),
        cost_estimate=pl.CostEstimate(
            flops=2 * 2 * 2048 * 8448 * HD, bytes_accessed=2 << 20, transcendentals=2048 * 8448
        ),
    )(
        query_proj,
        key_value,
        jnp.asarray(row_table),
        query_gain,
        key_gain,
        doc_offsets,
        jnp.asarray(base_table),
    )


def solution(mesh):
    placed = (P("ctx", "head"), P("ctx", "head"), P(), P(), P())
    return jax.shard_map(
        per_device, mesh=mesh, in_specs=placed, out_specs=P("ctx", "head"), check_vma=False
    )
```
